32 devices in a mesh: ctx: 4 (over y, x), fsdp: 8 (over z, core).
Axes of the slice: x: 2, y: 2, z: 4, core: 2. Of those that a mesh axis runs over, the one named last changes fastest.
Arguments:
- block_pos: int32 [2, 4], P(None, 'ctx'), may hold values from 0 to 3, each once within a row
- queries: bfloat16 [8, 512, 640], P('fsdp', 'ctx'), may hold values from -6 to 6
- keys: bfloat16 [8, 512, 128], P('fsdp', 'ctx'), may hold values from -6 to 6
- values: bfloat16 [8, 512, 128], P('fsdp', 'ctx'), may hold values from -12 to 12
- attention_output: bfloat16 [8, 512, 640], P('fsdp', 'ctx'), may hold values from -6 to 6
- output_gradient: bfloat16 [8, 512, 640], P('fsdp', 'ctx'), may hold values from -24 to 24
- log_softmax_norm: float32 [8, 5, 512], P('fsdp', None, 'ctx'), may hold values from 6 to 9
- features: bfloat16 [2, 512, 2560], P(None, 'ctx', 'fsdp'), may hold values from -0.119628906 to 0.119628906
Outputs:
- grad_q: bfloat16 [8, 512, 640], P('fsdp', 'ctx')
- key_gradient: bfloat16 [8, 512, 128], P('fsdp', 'ctx')
- value_gradient: bfloat16 [8, 512, 128], P('fsdp', 'ctx')
- grad_wk: float32 [2560, 512], P('fsdp')
The draws below stay inside these ranges and needn't reach their ends.
Inputs may be any that keep to these rules, and one draw needn't show every extreme that they name: Each row of block_pos holds every block place 0 to 3 once.
All inputs are finite; a program needn't handle non-finite values.
Results may differ from the reference program's by a relative error of at most 0.0058.
Values may be sent and summed in bfloat16 or wider, within the bound.
A program may use at most 64 MiB of HBM per device.

```python
import jax
import jax.numpy as jnp
from jax import lax

QUERY_HEADS = 20
KEY_VALUE_HEADS = 4
HEAD_SIZE = 128
HEAD_GROUPS = 4
DW = 2560
BLOCK_TOKENS = 128
SEQUENCE_COUNT = 2
SEQUENCE_TOKENS = 512
N_CTX = 4


def level_of(key, shape, pieces, low, top_value):
    factor_of = 1.0
    for axis_at, shards_of in pieces:
        draws = jax.random.uniform(jax.random.fold_in(jax.random.fold_in(key, 6), axis_at), (shards_of,), jnp.float32, low / len(pieces), top_value / len(pieces))
        factor_of = factor_of * jnp.repeat(jnp.exp(draws), shape[axis_at] // shards_of).reshape((-1,) + (1,) * (len(shape) - 1 - axis_at))
    return factor_of


def centred(stream_key, dims, width, bound, cuts=(), kind=jnp.bfloat16):
    values = width * jax.random.normal(stream_key, dims, jnp.float32)
    if cuts:
        values = values * level_of(stream_key, dims, cuts, -0.22, 0.18)
    return jnp.clip(values, -bound, bound).astype(kind)


def setup_inputs(seed: int = 0) -> dict:
    streams_of = jax.random.split(jax.random.key(seed), 9)
    return {
        "block_pos": jax.vmap(lambda own: jax.random.permutation(own, N_CTX))(jax.random.split(streams_of[0], SEQUENCE_COUNT)).reshape((SEQUENCE_COUNT, N_CTX)).astype(jnp.int32),
        "queries": centred(streams_of[1], (SEQUENCE_COUNT * HEAD_GROUPS, SEQUENCE_TOKENS, (QUERY_HEADS // HEAD_GROUPS) * HEAD_SIZE), 1.0, 6.0, ((0, 8), (1, 4))),
        "keys": centred(streams_of[2], (SEQUENCE_COUNT * HEAD_GROUPS, SEQUENCE_TOKENS, (KEY_VALUE_HEADS // HEAD_GROUPS) * HEAD_SIZE), 1.0, 6.0, ((0, 8), (1, 4))),
        "values": centred(streams_of[3], (SEQUENCE_COUNT * HEAD_GROUPS, SEQUENCE_TOKENS, (KEY_VALUE_HEADS // HEAD_GROUPS) * HEAD_SIZE), 2.0, 12.0, ((0, 8), (1, 4))),
        "attention_output": centred(streams_of[4], (SEQUENCE_COUNT * HEAD_GROUPS, SEQUENCE_TOKENS, (QUERY_HEADS // HEAD_GROUPS) * HEAD_SIZE), 1.0, 6.0, ((0, 8), (1, 4))),
        "output_gradient": centred(streams_of[5], (SEQUENCE_COUNT * HEAD_GROUPS, SEQUENCE_TOKENS, (QUERY_HEADS // HEAD_GROUPS) * HEAD_SIZE), 4.0, 24.0, ((0, 8), (1, 4))),
        "log_softmax_norm": jnp.clip(6.0 + 3.0 * jax.random.uniform(streams_of[6], (SEQUENCE_COUNT * HEAD_GROUPS, QUERY_HEADS // HEAD_GROUPS, SEQUENCE_TOKENS), jnp.float32) ** level_of(streams_of[6], (SEQUENCE_COUNT * HEAD_GROUPS, QUERY_HEADS // HEAD_GROUPS, SEQUENCE_TOKENS), ((0, 8), (2, 4)), -0.2, 0.2), 6.0, 9.0),
        "features": centred(streams_of[7], (SEQUENCE_COUNT, SEQUENCE_TOKENS, DW), 0.02, 0.119628906, ((1, 4), (2, 8))),
    }


def low_round(value):
    return lax.optimization_barrier(value.astype(jnp.bfloat16)).astype(jnp.float32)


def one_row(inputs):
    block_row, queries, keys, values, attention_output, output_gradient, log_softmax_norm = inputs
    sequence_length = queries.shape[0]
    kv_local = KEY_VALUE_HEADS // HEAD_GROUPS
    group_size = QUERY_HEADS // KEY_VALUE_HEADS
    score_scale = HEAD_SIZE ** -0.5
    offsets = jnp.arange(BLOCK_TOKENS, dtype=jnp.int32)
    positions = (block_row[:, None] * BLOCK_TOKENS + offsets[None, :]).reshape(sequence_length)
    visible = positions[None, :] <= positions[:, None]
    heads_of_queries = queries.astype(jnp.float32).reshape(sequence_length, kv_local, group_size, HEAD_SIZE).transpose(1, 0, 2, 3)
    head_gradient = output_gradient.astype(jnp.float32).reshape(sequence_length, kv_local, group_size, HEAD_SIZE).transpose(1, 0, 2, 3)
    heads_of_output = attention_output.astype(jnp.float32).reshape(sequence_length, kv_local, group_size, HEAD_SIZE).transpose(1, 0, 2, 3)
    heads_of_keys = keys.astype(jnp.float32).reshape(sequence_length, kv_local, HEAD_SIZE).transpose(1, 0, 2)
    heads_of_values = values.astype(jnp.float32).reshape(sequence_length, kv_local, HEAD_SIZE).transpose(1, 0, 2)
    heads_of_norm = log_softmax_norm.reshape(kv_local, group_size, sequence_length)

    def per_head(head_inputs):
        query_one, grad_one, out_one, key_one, value_one, norm_one = head_inputs
        delta = jnp.sum(grad_one * out_one, axis=-1)
        scores = jnp.einsum("tgd,ud->gtu", query_one, key_one) * score_scale
        soft_probs = jnp.where(visible[None], jnp.exp(scores - norm_one[:, :, None]), 0.0)
        dprobs = jnp.einsum("tgd,ud->gtu", grad_one, value_one)
        dscores = low_round(soft_probs * (dprobs - delta.T[:, :, None]) * score_scale)
        probs_low = low_round(soft_probs)
        grad_query = jnp.einsum("gtu,ud->tgd", dscores, key_one)
        gradient_for_key = jnp.einsum("gtu,tgd->ud", dscores, query_one)
        gradient_for_value = jnp.einsum("gtu,tgd->ud", probs_low, grad_one)
        return grad_query, gradient_for_key, gradient_for_value

    grad_query, gradient_for_key, gradient_for_value = lax.map(
        per_head, (heads_of_queries, head_gradient, heads_of_output, heads_of_keys, heads_of_values, heads_of_norm))
    grad_q = grad_query.transpose(1, 0, 2, 3).reshape(sequence_length, -1).astype(jnp.bfloat16)
    key_gradient = gradient_for_key.transpose(1, 0, 2).reshape(sequence_length, -1).astype(jnp.bfloat16)
    value_gradient = gradient_for_value.transpose(1, 0, 2).reshape(sequence_length, -1).astype(jnp.bfloat16)
    return grad_q, key_gradient, value_gradient


def weight_for_sequence(inputs):
    features, key_rows = inputs
    local_width = key_rows.shape[-1]
    feature_blocks = features.astype(jnp.float32).reshape(N_CTX, BLOCK_TOKENS, DW)
    key_blocks = key_rows.astype(jnp.float32).reshape(HEAD_GROUPS, N_CTX, BLOCK_TOKENS, local_width)
    key_blocks = key_blocks.transpose(1, 2, 0, 3).reshape(N_CTX, BLOCK_TOKENS, HEAD_GROUPS * local_width)
    partials = jnp.einsum("cti,ctj->cij", feature_blocks, key_blocks)
    return jnp.sum(low_round(partials), axis=0)


def reference(block_pos, queries, keys, values, attention_output, output_gradient, log_softmax_norm, features):
    block_rows = jnp.repeat(block_pos, HEAD_GROUPS, axis=0)
    grad_q, key_gradient, value_gradient = lax.map(
        one_row, (block_rows, queries, keys, values, attention_output, output_gradient, log_softmax_norm))
    key_by_sequence = key_gradient.reshape(SEQUENCE_COUNT, HEAD_GROUPS, SEQUENCE_TOKENS, key_gradient.shape[-1])
    weight_parts = lax.map(weight_for_sequence, (features, key_by_sequence))
    return grad_q, key_gradient, value_gradient, jnp.sum(weight_parts, axis=0)
```

```python
import functools

import jax
import jax.numpy as jnp
from jax import lax
from jax.experimental import pallas as pl
from jax.experimental.pallas import tpu as pltpu
from jax.sharding import PartitionSpec as P

QUERY_HEADS = 20
KEY_VALUE_HEADS = 4
HEAD_SIZE = 128
HEAD_GROUPS = 4
PLACE_ROWS = 16

F32 = jnp.float32
BF16 = jnp.bfloat16


def flipped(index, bits, count):
    total, unit = 0, 1
    while unit < count:
        digit = lax.rem(index // unit + (bits // unit) % 2, 2)
        total = total + digit * unit
        unit *= 2
    return total


def dot(a, b, contract):
    return lax.dot_general(a, b, ((contract[:1], contract[1:]), ((), ())), preferred_element_type=F32)


def kernel(
    n_ctx,
    n_fsdp,
    reducers,
    pos_ref,
    q_ref,
    k_ref,
    v_ref,
    o_ref,
    do_ref,
    lse_ref,
    x_ref,
    gq_ref,
    gk_ref,
    gv_ref,
    gw_ref,
    kv,
    qs,
    dos,
    ds,
    part_k,
    part_v,
    got_k,
    got_v,
    acc_k,
    acc_v,
    dk_all,
    x_t,
    rs_out,
    rs_in,
    ag_out,
    ag_in,
    kv_s,
    kv_r,
    pk_s,
    pk_r,
    pv_s,
    pv_r,
    dk_s,
    dk_r,
    rs_s,
    rs_r,
    ag_s,
    ag_r,
):
    rows = k_ref.shape[1]
    heads = q_ref.shape[2] // HEAD_SIZE
    seqs = x_ref.shape[0]
    scale = HEAD_SIZE ** (-0.5)
    c = lax.axis_index("ctx")
    f = lax.axis_index("fsdp")
    ctx_peers = {d: flipped(c, d, n_ctx) for d in range(1, n_ctx)}
    fsdp_peers = {e: flipped(f, e, n_fsdp) for e in range(1, n_fsdp)}
    direct = [e for e in range(1, n_fsdp) if e == 1 or e % 2 == 0]

    def remote(src, dst, send, recv, device):
        return pltpu.make_async_remote_copy(
            src_ref=src,
            dst_ref=dst,
            send_sem=send,
            recv_sem=recv,
            device_id=device,
            device_id_type=pl.DeviceIdType.MESH,
        )

    barrier = pltpu.get_barrier_semaphore()
    for d in range(1, n_ctx):
        pl.semaphore_signal(
            barrier, inc=1, device_id=(ctx_peers[d], f), device_id_type=pl.DeviceIdType.MESH
        )
    for e in direct:
        pl.semaphore_signal(
            barrier, inc=1, device_id=(c, fsdp_peers[e]), device_id_type=pl.DeviceIdType.MESH
        )
    place = pos_ref[f // HEAD_GROUPS, 0].astype(F32)
    kv[0, :rows] = k_ref[0]
    kv[0, rows : 2 * rows] = v_ref[0]
    kv[0, 2 * rows :] = jnp.full((PLACE_ROWS, HEAD_SIZE), place, F32).astype(BF16)
    pl.semaphore_wait(barrier, n_ctx - 1 + len(direct))

    kv_copies = {}
    for d in range(1, n_ctx):
        kv_copies[d] = remote(kv.at[0], kv.at[d], kv_s.at[d], kv_r.at[d], (ctx_peers[d], f))
        kv_copies[d].start()

    delta = []
    for h in range(heads):
        cols = slice(h * HEAD_SIZE, (h + 1) * HEAD_SIZE)
        qs[h * rows : (h + 1) * rows] = q_ref[0, :, cols]
        dos[h * rows : (h + 1) * rows] = do_ref[0, :, cols]
        product = do_ref[0, :, cols].astype(F32) * o_ref[0, :, cols].astype(F32)
        delta.append(jnp.sum(product.T, axis=0, keepdims=True))
    delta = jnp.concatenate(delta, axis=1)
    norms = lse_ref[0]
    norm = jnp.concatenate([norms[h : h + 1] for h in range(heads)], axis=1)
    token = lax.broadcasted_iota(jnp.int32, (1, rows), 1).astype(F32)
    key_row = lax.broadcasted_iota(jnp.int32, (rows, heads * rows), 0).astype(F32)

    def visit(d):
        key = kv[d, :rows]
        value = kv[d, rows : 2 * rows]
        key_place = jnp.max(kv[d, 2 * rows :].astype(F32), axis=0, keepdims=True)
        limit = token + (place - key_place) * rows
        visible = key_row <= jnp.concatenate([limit] * heads, axis=1)
        scores = dot(key, qs[...], (1, 1)) * scale
        probs = jnp.where(visible, jnp.exp(scores - norm), 0.0)
        dprobs = dot(value, dos[...], (1, 1))
        dscores = (probs * (dprobs - delta) * scale).astype(BF16)
        ds[d * rows : (d + 1) * rows] = dscores
        return dot(dscores, qs[...], (1, 0)), lambda: dot(probs.astype(BF16), dos[...], (1, 0))

    own_k, own_v = visit(0)
    acc_k[...] = own_k
    acc_v[...] = own_v()
    for s in range(seqs):
        x_t[:, s * rows : (s + 1) * rows] = x_ref[s].T

    pk_copies, pv_copies = {}, {}
    for d in range(1, n_ctx):
        kv_copies[d].wait_recv()
        to_k, to_v = visit(d)
        device = (ctx_peers[d], f)
        part_k[d] = to_k.astype(BF16)
        pk_copies[d] = remote(part_k.at[d], got_k.at[d], pk_s.at[d], pk_r.at[d], device)
        pk_copies[d].start()
        part_v[d] = to_v().astype(BF16)
        pv_copies[d] = remote(part_v.at[d], got_v.at[d], pv_s.at[d], pv_r.at[d], device)
        pv_copies[d].start()

    keys_all = jnp.concatenate([kv[d, :rows] for d in range(n_ctx)], axis=0)
    for h in range(heads):
        cols = slice(h * HEAD_SIZE, (h + 1) * HEAD_SIZE)
        gq_ref[0, :, cols] = dot(ds[:, cols], keys_all, (0, 0)).astype(BF16)

    dk = acc_k[...]
    for d in range(1, n_ctx):
        pk_copies[d].wait_recv()
        dk = dk + got_k[d].astype(F32)
    dk_low = dk.astype(BF16)
    gk_ref[0] = dk_low

    def slot(index):
        start = pl.multiple_of((index // HEAD_GROUPS) * rows, rows)
        return dk_all.at[lax.rem(index, HEAD_GROUPS), pl.ds(start, rows)]

    own_slot = slot(f)
    own_slot[...] = dk_low
    dk_copies = {}
    for e in direct:
        dk_copies[e] = remote(own_slot, own_slot, dk_s.at[e], dk_r.at[e], (c, fsdp_peers[e]))
        dk_copies[e].start()
    dv = acc_v[...]
    for d in range(1, n_ctx):
        pv_copies[d].wait_recv()
        dv = dv + got_v[d].astype(F32)
    gv_ref[0] = dv.astype(BF16)

    def arrived(e):
        there = slot(fsdp_peers[e])
        remote(there, there, dk_s.at[e], dk_r.at[e], (c, fsdp_peers[1])).wait_recv()

    for e in direct[1:]:
        arrived(e)
        there = slot(fsdp_peers[e])
        dk_copies[e + 1] = remote(
            there, there, dk_s.at[e + 1], dk_r.at[e + 1], (c, fsdp_peers[1])
        )
        dk_copies[e + 1].start()
    arrived(1)
    for e in direct[1:]:
        arrived(e + 1)

    width = gw_ref.shape[1] // reducers

    def chunk(owner):
        per = HEAD_SIZE
        groups = width // per
        parts = [dot(x_t[...], dk_all[owner * groups + g], (1, 0)) for g in range(groups)]
        return parts[0] if groups == 1 else jnp.concatenate(parts, axis=1)

    def columns(owner):
        return pl.ds(pl.multiple_of(owner * width, width), width)

    def guarded(index):
        if reducers == n_ctx:
            return lambda body: body()
        return pl.when(index < reducers)

    def rs_copy(d):
        return remote(rs_out.at[d], rs_in.at[d], rs_s.at[d], rs_r.at[d], (ctx_peers[d], f))

    def ag_copy(d):
        return remote(ag_out, ag_in.at[d], ag_s.at[d], ag_r.at[d], (ctx_peers[d], f))

    for d in range(1, n_ctx):

        @guarded(ctx_peers[d])
        def _():
            rs_out[d] = chunk(ctx_peers[d]).astype(BF16)
            rs_copy(d).start()

    @guarded(c)
    def _():
        total = chunk(c)
        for d in range(1, n_ctx):
            rs_copy(d).wait_recv()
            total = total + rs_in[d].astype(F32)
        low = total.astype(BF16)
        ag_out[...] = low
        for d in range(1, n_ctx):
            ag_copy(d).start()
        gw_ref[:, columns(c)] = low.astype(F32)

    for d in range(1, n_ctx):

        @guarded(ctx_peers[d])
        def _():
            ag_copy(d).wait_recv()
            gw_ref[:, columns(ctx_peers[d])] = ag_in[d].astype(F32)
            rs_copy(d).wait_send()

        @guarded(c)
        def _():
            ag_copy(d).wait_send()

        kv_copies[d].wait_send()
        pk_copies[d].wait_send()
        pv_copies[d].wait_send()
    for e in dk_copies:
        dk_copies[e].wait_send()


def local(n_ctx, n_fsdp, *args):
    queries, keys, features = args[1], args[2], args[7]
    rows = keys.shape[1]
    seqs, _, cols = features.shape
    heads = queries.shape[2] // HEAD_SIZE
    total = HEAD_GROUPS * keys.shape[2]
    reducers = min(n_ctx, HEAD_GROUPS)
    width = total // reducers
    vmem = pl.BlockSpec(memory_space=pltpu.VMEM)
    dma = pltpu.SemaphoreType.DMA
    return pl.pallas_call(
        functools.partial(kernel, n_ctx, n_fsdp, reducers),
        out_shape=(
            jax.ShapeDtypeStruct(queries.shape, BF16),
            jax.ShapeDtypeStruct(keys.shape, BF16),
            jax.ShapeDtypeStruct(keys.shape, BF16),
            jax.ShapeDtypeStruct((cols, total), F32),
        ),
        in_specs=[pl.BlockSpec(memory_space=pltpu.SMEM)] + [vmem] * 7,
        out_specs=(vmem,) * 4,
        scratch_shapes=[
            pltpu.VMEM((n_ctx, 2 * rows + PLACE_ROWS, HEAD_SIZE), BF16),
            pltpu.VMEM((heads * rows, HEAD_SIZE), BF16),
            pltpu.VMEM((heads * rows, HEAD_SIZE), BF16),
            pltpu.VMEM((n_ctx * rows, heads * rows), BF16),
            pltpu.VMEM((n_ctx, rows, HEAD_SIZE), BF16),
            pltpu.VMEM((n_ctx, rows, HEAD_SIZE), BF16),
            pltpu.VMEM((n_ctx, rows, HEAD_SIZE), BF16),
            pltpu.VMEM((n_ctx, rows, HEAD_SIZE), BF16),
            pltpu.VMEM((rows, HEAD_SIZE), F32),
            pltpu.VMEM((rows, HEAD_SIZE), F32),
            pltpu.VMEM((HEAD_GROUPS, seqs * rows, HEAD_SIZE), BF16),
            pltpu.VMEM((cols, seqs * rows), BF16),
            pltpu.VMEM((n_ctx, cols, width), BF16),
            pltpu.VMEM((n_ctx, cols, width), BF16),
            pltpu.VMEM((cols, width), BF16),
            pltpu.VMEM((n_ctx, cols, width), BF16),
        ]
        + [dma((n_ctx,))] * 6
        + [dma((n_fsdp,))] * 2
        + [dma((n_ctx,))] * 4,
        compiler_params=pltpu.CompilerParams(
            collective_id=0, has_side_effects=True, vmem_limit_bytes=40 * 1024 * 1024
        ),
    )(*args)


def solution(mesh):
    return jax.shard_map(
        functools.partial(local, mesh.shape["ctx"], mesh.shape["fsdp"]),
        mesh=mesh,
        in_specs=(
            P(None, "ctx"),
            P("fsdp", "ctx", None),
            P("fsdp", "ctx", None),
            P("fsdp", "ctx", None),
            P("fsdp", "ctx", None),
            P("fsdp", "ctx", None),
            P("fsdp", None, "ctx"),
            P(None, "ctx", "fsdp"),
        ),
        out_specs=(
            P("fsdp", "ctx", None),
            P("fsdp", "ctx", None),
            P("fsdp", "ctx", None),
            P("fsdp", None),
        ),
        check_vma=False,
    )
```

```python
import functools

import jax
import jax.numpy as jnp
from jax import lax
from jax.experimental import pallas as pl
from jax.experimental.pallas import tpu as pltpu
from jax.sharding import PartitionSpec as P

QUERY_HEADS = 20
KEY_VALUE_HEADS = 4
HEAD_SIZE = 128
HEAD_GROUPS = 4
PLACE_ROWS = 16

F32 = jnp.float32
BF16 = jnp.bfloat16


def flipped(index, bits, count):
    total, unit = 0, 1
    while unit < count:
        digit = lax.rem(index // unit + (bits // unit) % 2, 2)
        total = total + digit * unit
        unit *= 2
    return total


def dot(a, b, contract):
    return lax.dot_general(a, b, ((contract[:1], contract[1:]), ((), ())), preferred_element_type=F32)


def kernel(
    n_ctx,
    n_fsdp,
    reducers,
    pos_ref,
    q_ref,
    k_ref,
    v_ref,
    o_ref,
    do_ref,
    lse_ref,
    x_ref,
    gq_ref,
    gk_ref,
    gv_ref,
    gw_ref,
    kv,
    qs,
    dos,
    ds,
    part_k,
    part_v,
    got_k,
    got_v,
    acc_k,
    acc_v,
    dk_all,
    x_t,
    rs_out,
    rs_in,
    ag_out,
    ag_in,
    kv_s,
    kv_r,
    pk_s,
    pk_r,
    pv_s,
    pv_r,
    dk_s,
    dk_r,
    rs_s,
    rs_r,
    ag_s,
    ag_r,
    pos,
    q_in,
    do_in,
    o_in,
    lse_in,
    in_s,
):
    rows = k_ref.shape[1]
    heads = q_ref.shape[2] // HEAD_SIZE
    seqs = x_ref.shape[0]
    features = x_ref.shape[1]
    scale = HEAD_SIZE ** (-0.5)
    c = lax.axis_index("ctx")
    f = lax.axis_index("fsdp")
    ctx_peers = {d: flipped(c, d, n_ctx) for d in range(1, n_ctx)}
    fsdp_peers = {e: flipped(f, e, n_fsdp) for e in range(1, n_fsdp)}
    direct = [e for e in range(1, n_fsdp) if e == 1 or e % 2 == 0]

    def remote(src, dst, send, recv, device):
        return pltpu.make_async_remote_copy(
            src_ref=src,
            dst_ref=dst,
            send_sem=send,
            recv_sem=recv,
            device_id=device,
            device_id_type=pl.DeviceIdType.MESH,
        )

    loads = [
        (k_ref.at[0], kv.at[0, pl.ds(0, rows)]),
        (v_ref.at[0], kv.at[0, pl.ds(rows, rows)]),
        (pos_ref, pos),
        (do_ref.at[0], do_in),
        (o_ref.at[0], o_in),
        (q_ref.at[0], q_in),
        (lse_ref, lse_in),
    ]
    loads += [(x_ref.at[s], x_t.at[:, pl.ds(s * rows, rows)]) for s in range(seqs)]
    loads = [pltpu.make_async_copy(a, b, in_s.at[i]) for i, (a, b) in enumerate(loads)]
    for load in loads:
        load.start()

    barrier = pltpu.get_barrier_semaphore()
    for d in range(1, n_ctx):
        pl.semaphore_signal(
            barrier, inc=1, device_id=(ctx_peers[d], f), device_id_type=pl.DeviceIdType.MESH
        )
    for e in direct:
        pl.semaphore_signal(
            barrier, inc=1, device_id=(c, fsdp_peers[e]), device_id_type=pl.DeviceIdType.MESH
        )
    for load in loads[:3]:
        load.wait()
    place = pos[0, f // HEAD_GROUPS].astype(F32)
    kv[0, 2 * rows :] = jnp.full((PLACE_ROWS, HEAD_SIZE), place, F32).astype(BF16)
    pl.semaphore_wait(barrier, n_ctx - 1 + len(direct))

    kv_copies = {}
    for d in range(1, n_ctx):
        kv_copies[d] = remote(kv.at[0], kv.at[d], kv_s.at[d], kv_r.at[d], (ctx_peers[d], f))
        kv_copies[d].start()

    for load in loads[3:7]:
        load.wait()
    delta = []
    for h in range(heads):
        cols = slice(h * HEAD_SIZE, (h + 1) * HEAD_SIZE)
        qs[h * rows : (h + 1) * rows] = q_in[:, cols]
        dos[h * rows : (h + 1) * rows] = do_in[:, cols]
        product = do_in[:, cols].astype(F32) * o_in[:, cols].astype(F32)
        delta.append(jnp.sum(product.T, axis=0, keepdims=True))
    delta = jnp.concatenate(delta, axis=1)
    norm = jnp.concatenate([lse_in[h] for h in range(heads)], axis=1)
    token = lax.broadcasted_iota(jnp.int32, (1, rows), 1).astype(F32)
    key_row = lax.broadcasted_iota(jnp.int32, (rows, heads * rows), 0).astype(F32)

    def visit(d):
        key = kv[d, :rows]
        value = kv[d, rows : 2 * rows]
        key_place = jnp.max(kv[d, 2 * rows :].astype(F32), axis=0, keepdims=True)
        limit = token + (place - key_place) * rows
        visible = key_row <= jnp.concatenate([limit] * heads, axis=1)
        scores = dot(key, qs[...], (1, 1)) * scale
        probs = jnp.where(visible, jnp.exp(scores - norm), 0.0)
        dprobs = dot(value, dos[...], (1, 1))
        dscores = (probs * (dprobs - delta) * scale).astype(BF16)
        ds[d * rows : (d + 1) * rows] = dscores
        return dot(dscores, qs[...], (1, 0)), lambda: dot(probs.astype(BF16), dos[...], (1, 0))

    own_k, own_v = visit(0)
    acc_k[...] = own_k
    acc_v[...] = own_v()

    pk_copies, pv_copies = {}, {}
    for d in range(1, n_ctx):
        kv_copies[d].wait_recv()
        to_k, to_v = visit(d)
        device = (ctx_peers[d], f)
        part_k[d] = to_k.astype(BF16)
        pk_copies[d] = remote(part_k.at[d], got_k.at[d], pk_s.at[d], pk_r.at[d], device)
        pk_copies[d].start()
        part_v[d] = to_v().astype(BF16)
        pv_copies[d] = remote(part_v.at[d], got_v.at[d], pv_s.at[d], pv_r.at[d], device)
        pv_copies[d].start()

    keys_all = jnp.concatenate([kv[d, :rows] for d in range(n_ctx)], axis=0)
    for h in range(heads):
        cols = slice(h * HEAD_SIZE, (h + 1) * HEAD_SIZE)
        gq_ref[0, :, cols] = dot(ds[:, cols], keys_all, (0, 0)).astype(BF16)

    dk = acc_k[...]
    for d in range(1, n_ctx):
        pk_copies[d].wait_recv()
        dk = dk + got_k[d].astype(F32)
    dk_low = dk.astype(BF16)
    gk_ref[0] = dk_low

    def slot(index):
        start = pl.multiple_of((index // HEAD_GROUPS) * rows, rows)
        return dk_all.at[lax.rem(index, HEAD_GROUPS), pl.ds(start, rows)]

    own_slot = slot(f)
    own_slot[...] = dk_low
    dk_copies = {}
    for e in direct:
        dk_copies[e] = remote(own_slot, own_slot, dk_s.at[e], dk_r.at[e], (c, fsdp_peers[e]))
        dk_copies[e].start()
    dv = acc_v[...]
    for d in range(1, n_ctx):
        pv_copies[d].wait_recv()
        dv = dv + got_v[d].astype(F32)
    gv_ref[0] = dv.astype(BF16)

    def arrived(e):
        there = slot(fsdp_peers[e])
        remote(there, there, dk_s.at[e], dk_r.at[e], (c, fsdp_peers[1])).wait_recv()

    for load in loads[7:]:
        load.wait()
    part = features // reducers
    half = HEAD_GROUPS // 2
    parity = lax.rem(f, 2)

    def rs_copy(p, d):
        i = p * n_ctx + d
        return remote(rs_out.at[p, ctx_peers[d]], rs_in.at[p, d], rs_s.at[i], rs_r.at[i], (ctx_peers[d], f))

    def ag_copy(p, d):
        i = p * n_ctx + d
        return remote(ag_out.at[p], ag_in.at[p, d], ag_s.at[i], ag_r.at[i], (ctx_peers[d], f))

    def when_reducer(index, body):
        if reducers == n_ctx:
            body()
        else:
            pl.when(index < reducers)(body)

    def group(p, j):
        return 2 * j + lax.rem(parity + p, 2)

    def spread(p):
        for j in range(half):
            sums = dot(x_t[...], dk_all[group(p, j)], (1, 0))
            for owner in range(reducers):
                rs_out[p, owner, j] = sums[owner * part : (owner + 1) * part].astype(BF16)
        for d in range(1, n_ctx):
            when_reducer(ctx_peers[d], lambda: rs_copy(p, d).start())

    def store(p, owner, pieces):
        for j in range(half):
            at = pl.ds(pl.multiple_of(owner * part, 8), part)
            columns = pl.ds(pl.multiple_of(group(p, j) * HEAD_SIZE, HEAD_SIZE), HEAD_SIZE)
            gw_ref[at, columns] = pieces[j].astype(F32)

    def reduce(p):
        def body():
            for d in range(1, n_ctx):
                rs_copy(p, d).wait_recv()
            for j in range(half):
                total = rs_out[p, c, j].astype(F32)
                for d in range(1, n_ctx):
                    total = total + rs_in[p, d, j].astype(F32)
                ag_out[p, j] = total.astype(BF16)
            for d in range(1, n_ctx):
                ag_copy(p, d).start()
            store(p, c, ag_out[p])

        when_reducer(c, body)

    def collect(p):
        for d in range(1, n_ctx):

            def body():
                ag_copy(p, d).wait_recv()
                store(p, ctx_peers[d], ag_in[p, d])

            when_reducer(ctx_peers[d], body)

    for e in direct[1:]:
        arrived(e)
        there = slot(fsdp_peers[e])
        dk_copies[e + 1] = remote(
            there, there, dk_s.at[e + 1], dk_r.at[e + 1], (c, fsdp_peers[1])
        )
        dk_copies[e + 1].start()
    spread(0)
    arrived(1)
    for e in direct[1:]:
        arrived(e + 1)
    spread(1)
    reduce(0)
    reduce(1)
    collect(0)
    collect(1)

    for d in range(1, n_ctx):
        for p in range(2):
            when_reducer(ctx_peers[d], lambda: rs_copy(p, d).wait_send())
            when_reducer(c, lambda: ag_copy(p, d).wait_send())
        kv_copies[d].wait_send()
        pk_copies[d].wait_send()
        pv_copies[d].wait_send()
    for e in dk_copies:
        dk_copies[e].wait_send()


def write_out(*refs):
    count = len(refs) // 2
    for i in range(count):
        refs[count + i][...] = refs[i][...]


def local(
    n_ctx, n_fsdp, block_pos, queries, keys, values, output, output_gradient, norm, features
):
    rows = keys.shape[1]
    seqs, _, cols = features.shape
    heads = queries.shape[2] // HEAD_SIZE
    total = HEAD_GROUPS * keys.shape[2]
    reducers = max(r for r in range(1, n_ctx + 1) if cols % (16 * r) == 0)
    part = cols // reducers
    half = HEAD_GROUPS // 2
    vmem = pl.BlockSpec(memory_space=pltpu.VMEM)
    hbm = pl.BlockSpec(memory_space=pltpu.HBM)
    dma = pltpu.SemaphoreType.DMA
    shapes = (
        jax.ShapeDtypeStruct(queries.shape, BF16),
        jax.ShapeDtypeStruct(keys.shape, BF16),
        jax.ShapeDtypeStruct(keys.shape, BF16),
        jax.ShapeDtypeStruct((cols, total), F32),
    )
    results = pl.pallas_call(
        functools.partial(kernel, n_ctx, n_fsdp, reducers),
        out_shape=shapes,
        in_specs=[hbm] * 8,
        out_specs=(vmem,) * 4,
        scratch_shapes=[
            pltpu.VMEM((n_ctx, 2 * rows + PLACE_ROWS, HEAD_SIZE), BF16),
            pltpu.VMEM((heads * rows, HEAD_SIZE), BF16),
            pltpu.VMEM((heads * rows, HEAD_SIZE), BF16),
            pltpu.VMEM((n_ctx * rows, heads * rows), BF16),
            pltpu.VMEM((n_ctx, rows, HEAD_SIZE), BF16),
            pltpu.VMEM((n_ctx, rows, HEAD_SIZE), BF16),
            pltpu.VMEM((n_ctx, rows, HEAD_SIZE), BF16),
            pltpu.VMEM((n_ctx, rows, HEAD_SIZE), BF16),
            pltpu.VMEM((rows, HEAD_SIZE), F32),
            pltpu.VMEM((rows, HEAD_SIZE), F32),
            pltpu.VMEM((HEAD_GROUPS, seqs * rows, HEAD_SIZE), BF16),
            pltpu.VMEM((cols, seqs * rows), BF16),
            pltpu.VMEM((2, n_ctx, half, part, HEAD_SIZE), BF16),
            pltpu.VMEM((2, n_ctx, half, part, HEAD_SIZE), BF16),
            pltpu.VMEM((2, half, part, HEAD_SIZE), BF16),
            pltpu.VMEM((2, n_ctx, half, part, HEAD_SIZE), BF16),
        ]
        + [dma((n_ctx,))] * 6
        + [dma((n_fsdp,))] * 2
        + [dma((2 * n_ctx,))] * 4
        + [
            pltpu.SMEM((1, seqs), jnp.int32),
            pltpu.VMEM(queries.shape[1:], BF16),
            pltpu.VMEM(queries.shape[1:], BF16),
            pltpu.VMEM(queries.shape[1:], BF16),
            pltpu.VMEM((heads, 1, rows), F32),
            dma((7 + seqs,)),
        ],
        compiler_params=pltpu.CompilerParams(
            collective_id=0, has_side_effects=True, vmem_limit_bytes=60 * 1024 * 1024
        ),
    )(
        block_pos.T,
        queries,
        keys,
        values,
        output,
        output_gradient,
        jnp.swapaxes(norm, 0, 1),
        jnp.swapaxes(features, 1, 2),
    )
    return pl.pallas_call(
        write_out,
        out_shape=shapes,
        in_specs=[vmem] * 4,
        out_specs=(vmem,) * 4,
    )(*results)


def solution(mesh):
    return jax.shard_map(
        functools.partial(local, mesh.shape["ctx"], mesh.shape["fsdp"]),
        mesh=mesh,
        in_specs=(
            P(None, "ctx"),
            P("fsdp", "ctx", None),
            P("fsdp", "ctx", None),
            P("fsdp", "ctx", None),
            P("fsdp", "ctx", None),
            P("fsdp", "ctx", None),
            P("fsdp", None, "ctx"),
            P(None, "ctx", "fsdp"),
        ),
        out_specs=(
            P("fsdp", "ctx", None),
            P("fsdp", "ctx", None),
            P("fsdp", "ctx", None),
            P("fsdp", None),
        ),
        check_vma=False,
    )
```

```python
import functools

import jax
import jax.numpy as jnp
from jax import lax
from jax.experimental import pallas as pl
from jax.experimental.pallas import tpu as pltpu
from jax.sharding import PartitionSpec as P

QUERY_HEADS = 20
KEY_VALUE_HEADS = 4
HEAD_SIZE = 128
HEAD_GROUPS = 4
PLACE_ROWS = 16

F32 = jnp.float32
BF16 = jnp.bfloat16


def flipped(index, bits, count):
    total, unit = 0, 1
    while unit < count:
        digit = lax.rem(index // unit + (bits // unit) % 2, 2)
        total = total + digit * unit
        unit *= 2
    return total


def dot(a, b, contract):
    return lax.dot_general(a, b, ((contract[:1], contract[1:]), ((), ())), preferred_element_type=F32)


def kernel(
    n_ctx,
    n_fsdp,
    reducers,
    pos_ref,
    q_ref,
    k_ref,
    v_ref,
    o_ref,
    do_ref,
    lse_ref,
    x_ref,
    gq_out,
    gk_out,
    gv_out,
    gw_out,
    kv,
    qs,
    dos,
    ds,
    part_k,
    part_v,
    got_k,
    got_v,
    acc_k,
    acc_v,
    dk_all,
    x_t,
    rs_out,
    rs_in,
    ag_out,
    kv_s,
    kv_r,
    pk_s,
    pk_r,
    pv_s,
    pv_r,
    dk_s,
    dk_r,
    rs_s,
    rs_r,
    ag_s,
    ag_r,
    pos,
    q_in,
    do_in,
    o_in,
    lse_in,
    in_s,
    gq_ref,
    gk_ref,
    gv_ref,
    ps,
    out_s,
):
    rows = k_ref.shape[1]
    heads = q_ref.shape[2] // HEAD_SIZE
    seqs = x_ref.shape[0]
    features = x_ref.shape[1]
    scale = HEAD_SIZE ** (-0.5)
    c = lax.axis_index("ctx")
    f = lax.axis_index("fsdp")
    ctx_peers = {d: flipped(c, d, n_ctx) for d in range(1, n_ctx)}
    fsdp_peers = {e: flipped(f, e, n_fsdp) for e in range(1, n_fsdp)}
    direct = [e for e in range(1, n_fsdp) if e == 1 or e % 2 == 0]

    def remote(src, dst, send, recv, device):
        return pltpu.make_async_remote_copy(
            src_ref=src,
            dst_ref=dst,
            send_sem=send,
            recv_sem=recv,
            device_id=device,
            device_id_type=pl.DeviceIdType.MESH,
        )

    barrier = pltpu.get_barrier_semaphore()
    for d in range(1, n_ctx):
        pl.semaphore_signal(
            barrier, inc=1, device_id=(ctx_peers[d], f), device_id_type=pl.DeviceIdType.MESH
        )
    for e in direct:
        pl.semaphore_signal(
            barrier, inc=1, device_id=(c, fsdp_peers[e]), device_id_type=pl.DeviceIdType.MESH
        )
    loads = [
        (k_ref.at[0], kv.at[0, pl.ds(0, rows)]),
        (v_ref.at[0], kv.at[0, pl.ds(rows, rows)]),
        (pos_ref, pos),
        (do_ref.at[0], do_in),
        (o_ref.at[0], o_in),
        (q_ref.at[0], q_in),
        (lse_ref, lse_in),
    ]
    loads += [(x_ref.at[s], x_t.at[:, pl.ds(s * rows, rows)]) for s in range(seqs)]
    loads = [pltpu.make_async_copy(a, b, in_s.at[i]) for i, (a, b) in enumerate(loads)]
    for load in loads:
        load.start()

    writes = [
        pltpu.make_async_copy(a, b, out_s.at[i])
        for i, (a, b) in enumerate([(gq_ref, gq_out), (gk_ref, gk_out), (gv_ref, gv_out)])
    ]
    for load in loads[:3]:
        load.wait()
    place = pos[0, f // HEAD_GROUPS].astype(F32)
    kv[0, 2 * rows :] = jnp.full((PLACE_ROWS, HEAD_SIZE), place, F32).astype(BF16)
    pl.semaphore_wait(barrier, n_ctx - 1 + len(direct))

    kv_copies = {}
    for d in range(1, n_ctx):
        kv_copies[d] = remote(kv.at[0], kv.at[d], kv_s.at[d], kv_r.at[d], (ctx_peers[d], f))
        kv_copies[d].start()

    for load in loads[3:7]:
        load.wait()
    delta = []
    for h in range(heads):
        cols = slice(h * HEAD_SIZE, (h + 1) * HEAD_SIZE)
        qs[h * rows : (h + 1) * rows] = q_in[:, cols]
        dos[h * rows : (h + 1) * rows] = do_in[:, cols]
        product = do_in[:, cols].astype(F32) * o_in[:, cols].astype(F32)
        delta.append(jnp.sum(product.T, axis=0, keepdims=True))
    delta = jnp.concatenate(delta, axis=1)
    norm = jnp.concatenate([lse_in[h] for h in range(heads)], axis=1)
    token = lax.broadcasted_iota(jnp.int32, (1, rows), 1).astype(F32)
    key_row = lax.broadcasted_iota(jnp.int32, (rows, heads * rows), 0).astype(F32)

    def visit(d):
        key = kv[d, :rows]
        value = kv[d, rows : 2 * rows]
        key_place = jnp.max(kv[d, 2 * rows :].astype(F32), axis=0, keepdims=True)
        limit = token + (place - key_place) * rows
        visible = key_row <= jnp.concatenate([limit] * heads, axis=1)
        scores = dot(key, qs[...], (1, 1)) * scale
        probs = jnp.where(visible, jnp.exp(scores - norm), 0.0)
        dprobs = dot(value, dos[...], (1, 1))
        dscores = (probs * (dprobs - delta) * scale).astype(BF16)
        ds[d * rows : (d + 1) * rows] = dscores
        ps[d * rows : (d + 1) * rows] = probs.astype(BF16)
        return dot(dscores, qs[...], (1, 0))

    def value_part(d):
        return dot(ps[d * rows : (d + 1) * rows], dos[...], (1, 0))

    acc_k[...] = visit(0)

    pk_copies, pv_copies = {}, {}
    for d in range(1, n_ctx):
        kv_copies[d].wait_recv()
        part_k[d] = visit(d).astype(BF16)
        pk_copies[d] = remote(
            part_k.at[d], got_k.at[d], pk_s.at[d], pk_r.at[d], (ctx_peers[d], f)
        )
        pk_copies[d].start()
    for d in range(1, n_ctx):
        part_v[d] = value_part(d).astype(BF16)
        pv_copies[d] = remote(
            part_v.at[d], got_v.at[d], pv_s.at[d], pv_r.at[d], (ctx_peers[d], f)
        )
        pv_copies[d].start()
    acc_v[...] = value_part(0)

    keys_all = jnp.concatenate([kv[d, :rows] for d in range(n_ctx)], axis=0)
    for h in range(heads):
        cols = slice(h * HEAD_SIZE, (h + 1) * HEAD_SIZE)
        gq_ref[0, :, cols] = dot(ds[:, cols], keys_all, (0, 0)).astype(BF16)

    writes[0].start()

    dk = acc_k[...]
    for d in range(1, n_ctx):
        pk_copies[d].wait_recv()
        dk = dk + got_k[d].astype(F32)
    dk_low = dk.astype(BF16)
    gk_ref[0] = dk_low

    def slot(index):
        start = pl.multiple_of((index // HEAD_GROUPS) * rows, rows)
        return dk_all.at[lax.rem(index, HEAD_GROUPS), pl.ds(start, rows)]

    own_slot = slot(f)
    own_slot[...] = dk_low
    dk_copies = {}
    for e in direct:
        dk_copies[e] = remote(own_slot, own_slot, dk_s.at[e], dk_r.at[e], (c, fsdp_peers[e]))
        dk_copies[e].start()
    writes[1].start()
    dv = acc_v[...]
    for d in range(1, n_ctx):
        pv_copies[d].wait_recv()
        dv = dv + got_v[d].astype(F32)
    gv_ref[0] = dv.astype(BF16)
    writes[2].start()

    def arrived(e):
        there = slot(fsdp_peers[e])
        remote(there, there, dk_s.at[e], dk_r.at[e], (c, fsdp_peers[1])).wait_recv()

    for load in loads[7:]:
        load.wait()
    part = features // reducers
    half = HEAD_GROUPS // 2
    parity = lax.rem(f, 2)

    def rs_copy(p, d):
        i = p * n_ctx + d
        return remote(rs_out.at[p, ctx_peers[d]], rs_in.at[p, d], rs_s.at[i], rs_r.at[i], (ctx_peers[d], f))

    def region(p, owner):
        at = pl.ds(pl.multiple_of(owner * part, 16), part)
        return gw_out.at[lax.rem(parity + p, 2), :, at]

    def ag_copy(p, d, owner):
        i = p * n_ctx + d
        place_of = region(p, owner)
        return remote(ag_out.at[p], place_of, ag_s.at[i], ag_r.at[i], (ctx_peers[d], f))

    def own_copy(p):
        return pltpu.make_async_copy(ag_out.at[p], region(p, c), out_s.at[3 + p])

    def when_reducer(index, body):
        if reducers == n_ctx:
            body()
        else:
            pl.when(index < reducers)(body)

    def group(p, j):
        return 2 * j + lax.rem(parity + p, 2)

    def spread(p):
        for j in range(half):
            sums = dot(x_t[...], dk_all[group(p, j)], (1, 0))
            for owner in range(reducers):
                rs_out[p, owner, j] = sums[owner * part : (owner + 1) * part].astype(BF16)
        for d in range(1, n_ctx):
            when_reducer(ctx_peers[d], lambda: rs_copy(p, d).start())

    def reduce(p):
        def body():
            for d in range(1, n_ctx):
                rs_copy(p, d).wait_recv()
            for j in range(half):
                total = rs_out[p, c, j].astype(F32)
                for d in range(1, n_ctx):
                    total = total + rs_in[p, d, j].astype(F32)
                ag_out[p, j] = total.astype(BF16)
            for d in range(1, n_ctx):
                ag_copy(p, d, c).start()
            own_copy(p).start()

        when_reducer(c, body)

    def collect(p):
        for d in range(1, n_ctx):
            when_reducer(
                ctx_peers[d], lambda: ag_copy(p, d, ctx_peers[d]).wait_recv()
            )

    for e in direct[1:]:
        arrived(e)
        there = slot(fsdp_peers[e])
        dk_copies[e + 1] = remote(
            there, there, dk_s.at[e + 1], dk_r.at[e + 1], (c, fsdp_peers[1])
        )
        dk_copies[e + 1].start()
    spread(0)
    arrived(1)
    for e in direct[1:]:
        arrived(e + 1)
    spread(1)
    reduce(0)
    reduce(1)
    collect(0)
    collect(1)

    for d in range(1, n_ctx):
        for p in range(2):
            when_reducer(ctx_peers[d], lambda: rs_copy(p, d).wait_send())
            when_reducer(c, lambda: ag_copy(p, d, c).wait_send())
        kv_copies[d].wait_send()
        pk_copies[d].wait_send()
        pv_copies[d].wait_send()
    for e in dk_copies:
        dk_copies[e].wait_send()
    for write in writes:
        write.wait()
    for p in range(2):
        when_reducer(c, lambda: own_copy(p).wait())


def write_out(*refs):
    sources, targets, held = refs[:4], refs[4:8], refs[8:12]
    wide, in_s, out_s = refs[12:]
    loads = [pltpu.make_async_copy(sources[i], held[i], in_s.at[i]) for i in range(4)]
    stores = [
        pltpu.make_async_copy(wide if i == 3 else held[i], targets[i], out_s.at[i])
        for i in range(4)
    ]
    for i in (3, 0, 1, 2):
        loads[i].start()
    for i in range(3):
        loads[i].wait()
        stores[i].start()
    loads[3].wait()
    for group in range(HEAD_GROUPS):
        columns = slice(group * HEAD_SIZE, (group + 1) * HEAD_SIZE)
        wide[:, columns] = held[3][group % 2, group // 2].astype(F32)
    stores[3].start()
    for store in stores:
        store.wait()


def local(
    n_ctx, n_fsdp, block_pos, queries, keys, values, output, output_gradient, norm, features
):
    rows = keys.shape[1]
    seqs, _, cols = features.shape
    heads = queries.shape[2] // HEAD_SIZE
    total = HEAD_GROUPS * keys.shape[2]
    reducers = max(r for r in range(1, n_ctx + 1) if cols % (16 * r) == 0)
    part = cols // reducers
    half = HEAD_GROUPS // 2
    hbm = pl.BlockSpec(memory_space=pltpu.HBM)
    dma = pltpu.SemaphoreType.DMA
    shapes = (
        jax.ShapeDtypeStruct(queries.shape, BF16),
        jax.ShapeDtypeStruct(keys.shape, BF16),
        jax.ShapeDtypeStruct(keys.shape, BF16),
        jax.ShapeDtypeStruct((2, half, cols, HEAD_SIZE), BF16),
    )
    results = pl.pallas_call(
        functools.partial(kernel, n_ctx, n_fsdp, reducers),
        out_shape=shapes,
        in_specs=[hbm] * 8,
        out_specs=(hbm,) * 4,
        scratch_shapes=[
            pltpu.VMEM((n_ctx, 2 * rows + PLACE_ROWS, HEAD_SIZE), BF16),
            pltpu.VMEM((heads * rows, HEAD_SIZE), BF16),
            pltpu.VMEM((heads * rows, HEAD_SIZE), BF16),
            pltpu.VMEM((n_ctx * rows, heads * rows), BF16),
            pltpu.VMEM((n_ctx, rows, HEAD_SIZE), BF16),
            pltpu.VMEM((n_ctx, rows, HEAD_SIZE), BF16),
            pltpu.VMEM((n_ctx, rows, HEAD_SIZE), BF16),
            pltpu.VMEM((n_ctx, rows, HEAD_SIZE), BF16),
            pltpu.VMEM((rows, HEAD_SIZE), F32),
            pltpu.VMEM((rows, HEAD_SIZE), F32),
            pltpu.VMEM((HEAD_GROUPS, seqs * rows, HEAD_SIZE), BF16),
            pltpu.VMEM((cols, seqs * rows), BF16),
            pltpu.VMEM((2, n_ctx, half, part, HEAD_SIZE), BF16),
            pltpu.VMEM((2, n_ctx, half, part, HEAD_SIZE), BF16),
            pltpu.VMEM((2, half, part, HEAD_SIZE), BF16),
        ]
        + [dma((n_ctx,))] * 6
        + [dma((n_fsdp,))] * 2
        + [dma((2 * n_ctx,))] * 4
        + [
            pltpu.SMEM((1, seqs), jnp.int32),
            pltpu.VMEM(queries.shape[1:], BF16),
            pltpu.VMEM(queries.shape[1:], BF16),
            pltpu.VMEM(queries.shape[1:], BF16),
            pltpu.VMEM((heads, 1, rows), F32),
            dma((7 + seqs,)),
            pltpu.VMEM(queries.shape, BF16),
            pltpu.VMEM(keys.shape, BF16),
            pltpu.VMEM(keys.shape, BF16),
            pltpu.VMEM((n_ctx * rows, heads * rows), BF16),
            dma((5,)),
        ],
        compiler_params=pltpu.CompilerParams(
            collective_id=0, has_side_effects=True, vmem_limit_bytes=60 * 1024 * 1024
        ),
    )(
        block_pos.T,
        queries,
        keys,
        values,
        output,
        output_gradient,
        jnp.swapaxes(norm, 0, 1),
        jnp.swapaxes(features, 1, 2),
    )
    return pl.pallas_call(
        write_out,
        out_shape=(*shapes[:3], jax.ShapeDtypeStruct((cols, total), F32)),
        in_specs=[hbm] * 4,
        out_specs=(hbm,) * 4,
        scratch_shapes=[pltpu.VMEM(each.shape, each.dtype) for each in shapes]
        + [pltpu.VMEM((cols, total), F32), dma((4,)), dma((4,))],
    )(*results)


def solution(mesh):
    return jax.shard_map(
        functools.partial(local, mesh.shape["ctx"], mesh.shape["fsdp"]),
        mesh=mesh,
        in_specs=(
            P(None, "ctx"),
            P("fsdp", "ctx", None),
            P("fsdp", "ctx", None),
            P("fsdp", "ctx", None),
            P("fsdp", "ctx", None),
            P("fsdp", "ctx", None),
            P("fsdp", None, "ctx"),
            P(None, "ctx", "fsdp"),
        ),
        out_specs=(
            P("fsdp", "ctx", None),
            P("fsdp", "ctx", None),
            P("fsdp", "ctx", None),
            P("fsdp", None),
        ),
        check_vma=False,
    )
```

```python
import functools

import jax
import jax.numpy as jnp
from jax import lax
from jax.experimental import pallas as pl
from jax.experimental.pallas import tpu as pltpu
from jax.sharding import PartitionSpec as P

QUERY_HEADS = 20
KEY_VALUE_HEADS = 4
HEAD_SIZE = 128
HEAD_GROUPS = 4
PLACE_ROWS = 16

F32 = jnp.float32
BF16 = jnp.bfloat16


def flipped(index, bits, count):
    total, unit = 0, 1
    while unit < count:
        digit = lax.rem(index // unit + (bits // unit) % 2, 2)
        total = total + digit * unit
        unit *= 2
    return total


def dot(a, b, contract):
    return lax.dot_general(a, b, ((contract[:1], contract[1:]), ((), ())), preferred_element_type=F32)


def kernel(
    n_ctx,
    n_fsdp,
    reducers,
    pos_ref,
    q_ref,
    k_ref,
    v_ref,
    o_ref,
    do_ref,
    lse_ref,
    x_ref,
    gq_out,
    gk_out,
    gv_out,
    gw_out,
    kv,
    qs,
    dos,
    ds,
    part_k,
    part_v,
    got_k,
    got_v,
    acc_k,
    acc_v,
    dk_all,
    x_t,
    rs_out,
    rs_in,
    ag_out,
    kv_s,
    kv_r,
    pk_s,
    pk_r,
    pv_s,
    pv_r,
    dk_s,
    dk_r,
    rs_s,
    rs_r,
    ag_s,
    ag_r,
    pos,
    q_in,
    do_in,
    o_in,
    lse_in,
    in_s,
    gq_ref,
    gk_ref,
    gv_ref,
    ps,
    out_s,
):
    rows = k_ref.shape[1]
    heads = q_ref.shape[2] // HEAD_SIZE
    seqs = x_ref.shape[0]
    features = x_ref.shape[1]
    scale = HEAD_SIZE ** (-0.5)
    c = lax.axis_index("ctx")
    f = lax.axis_index("fsdp")
    ctx_peers = {d: flipped(c, d, n_ctx) for d in range(1, n_ctx)}
    fsdp_peers = {e: flipped(f, e, n_fsdp) for e in range(1, n_fsdp)}
    direct = [e for e in range(1, n_fsdp) if e == 1 or e % 2 == 0]

    def remote(src, dst, send, recv, device):
        return pltpu.make_async_remote_copy(
            src_ref=src,
            dst_ref=dst,
            send_sem=send,
            recv_sem=recv,
            device_id=device,
            device_id_type=pl.DeviceIdType.MESH,
        )

    barrier = pltpu.get_barrier_semaphore()
    for d in range(1, n_ctx):
        pl.semaphore_signal(
            barrier, inc=1, device_id=(ctx_peers[d], f), device_id_type=pl.DeviceIdType.MESH
        )
    for e in direct:
        pl.semaphore_signal(
            barrier, inc=1, device_id=(c, fsdp_peers[e]), device_id_type=pl.DeviceIdType.MESH
        )
    loads = [
        (k_ref.at[0], kv.at[0, pl.ds(0, rows)]),
        (v_ref.at[0], kv.at[0, pl.ds(rows, rows)]),
        (pos_ref, pos),
        (do_ref.at[0], do_in),
        (o_ref.at[0], o_in),
        (q_ref.at[0], q_in),
        (lse_ref, lse_in),
    ]
    loads += [(x_ref.at[s], x_t.at[:, pl.ds(s * rows, rows)]) for s in range(seqs)]
    loads = [pltpu.make_async_copy(a, b, in_s.at[i]) for i, (a, b) in enumerate(loads)]
    for load in loads:
        load.start()

    writes = [
        pltpu.make_async_copy(a, b, out_s.at[i])
        for i, (a, b) in enumerate([(gq_ref, gq_out), (gk_ref, gk_out), (gv_ref, gv_out)])
    ]
    for load in loads[:3]:
        load.wait()
    place = pos[0, f // HEAD_GROUPS].astype(F32)
    kv[0, 2 * rows :] = jnp.full((PLACE_ROWS, HEAD_SIZE), place, F32).astype(BF16)
    pl.semaphore_wait(barrier, n_ctx - 1 + len(direct))

    kv_copies = {}
    for d in reversed(range(1, n_ctx)):
        kv_copies[d] = remote(kv.at[0], kv.at[d], kv_s.at[d], kv_r.at[d], (ctx_peers[d], f))
        kv_copies[d].start()

    for load in loads[3:7]:
        load.wait()
    delta = []
    for h in range(heads):
        cols = slice(h * HEAD_SIZE, (h + 1) * HEAD_SIZE)
        qs[h * rows : (h + 1) * rows] = q_in[:, cols]
        dos[h * rows : (h + 1) * rows] = do_in[:, cols]
        product = do_in[:, cols].astype(F32) * o_in[:, cols].astype(F32)
        delta.append(jnp.sum(product.T, axis=0, keepdims=True))
    delta = jnp.concatenate(delta, axis=1)
    norm = jnp.concatenate([lse_in[h] for h in range(heads)], axis=1)
    token = lax.broadcasted_iota(jnp.int32, (1, rows), 1).astype(F32)
    key_row = lax.broadcasted_iota(jnp.int32, (rows, heads * rows), 0).astype(F32)

    def visit(d):
        key = kv[d, :rows]
        value = kv[d, rows : 2 * rows]
        key_place = jnp.max(kv[d, 2 * rows :].astype(F32), axis=0, keepdims=True)
        limit = token + (place - key_place) * rows
        visible = key_row <= jnp.concatenate([limit] * heads, axis=1)
        scores = dot(key, qs[...], (1, 1)) * scale
        probs = jnp.where(visible, jnp.exp(scores - norm), 0.0)
        dprobs = dot(value, dos[...], (1, 1))
        dscores = (probs * (dprobs - delta) * scale).astype(BF16)
        ds[d * rows : (d + 1) * rows] = dscores
        ps[d * rows : (d + 1) * rows] = probs.astype(BF16)
        return dot(dscores, qs[...], (1, 0))

    def value_part(d):
        return dot(ps[d * rows : (d + 1) * rows], dos[...], (1, 0))

    acc_k[...] = visit(0)

    pk_copies, pv_copies = {}, {}
    for d in range(1, n_ctx):
        kv_copies[d].wait_recv()
        part_k[d] = visit(d).astype(BF16)
        pk_copies[d] = remote(
            part_k.at[d], got_k.at[d], pk_s.at[d], pk_r.at[d], (ctx_peers[d], f)
        )
        pk_copies[d].start()
    for d in range(1, n_ctx):
        part_v[d] = value_part(d).astype(BF16)
        pv_copies[d] = remote(
            part_v.at[d], got_v.at[d], pv_s.at[d], pv_r.at[d], (ctx_peers[d], f)
        )
        pv_copies[d].start()
    acc_v[...] = value_part(0)

    keys_all = jnp.concatenate([kv[d, :rows] for d in range(n_ctx)], axis=0)
    for h in range(heads):
        cols = slice(h * HEAD_SIZE, (h + 1) * HEAD_SIZE)
        gq_ref[0, :, cols] = dot(ds[:, cols], keys_all, (0, 0)).astype(BF16)

    writes[0].start()

    dk = acc_k[...]
    for d in range(1, n_ctx):
        pk_copies[d].wait_recv()
        dk = dk + got_k[d].astype(F32)
    dk_low = dk.astype(BF16)
    gk_ref[0] = dk_low

    def slot(index):
        start = pl.multiple_of((index // HEAD_GROUPS) * rows, rows)
        return dk_all.at[lax.rem(index, HEAD_GROUPS), pl.ds(start, rows)]

    own_slot = slot(f)
    own_slot[...] = dk_low
    dk_copies = {}
    for e in reversed(direct):
        dk_copies[e] = remote(own_slot, own_slot, dk_s.at[e], dk_r.at[e], (c, fsdp_peers[e]))
        dk_copies[e].start()
    writes[1].start()
    dv = acc_v[...]
    for d in range(1, n_ctx):
        pv_copies[d].wait_recv()
        dv = dv + got_v[d].astype(F32)
    gv_ref[0] = dv.astype(BF16)
    writes[2].start()

    def arrived(e):
        there = slot(fsdp_peers[e])
        remote(there, there, dk_s.at[e], dk_r.at[e], (c, fsdp_peers[1])).wait_recv()

    for load in loads[7:]:
        load.wait()
    part = features // reducers
    half = HEAD_GROUPS // 2
    parity = lax.rem(f, 2)

    def rs_copy(p, d):
        i = p * n_ctx + d
        return remote(rs_out.at[p, ctx_peers[d]], rs_in.at[p, d], rs_s.at[i], rs_r.at[i], (ctx_peers[d], f))

    def region(p, owner):
        at = pl.ds(pl.multiple_of(owner * part, 16), part)
        return gw_out.at[lax.rem(parity + p, 2), :, at]

    def ag_copy(p, d, owner):
        i = p * n_ctx + d
        place_of = region(p, owner)
        return remote(ag_out.at[p], place_of, ag_s.at[i], ag_r.at[i], (ctx_peers[d], f))

    def own_copy(p):
        return pltpu.make_async_copy(ag_out.at[p], region(p, c), out_s.at[3 + p])

    def when_reducer(index, body):
        if reducers == n_ctx:
            body()
        else:
            pl.when(index < reducers)(body)

    def group(p, j):
        return 2 * j + lax.rem(parity + p, 2)

    def spread(p):
        for j in range(half):
            sums = dot(x_t[...], dk_all[group(p, j)], (1, 0))
            for owner in range(reducers):
                rs_out[p, owner, j] = sums[owner * part : (owner + 1) * part].astype(BF16)
        for d in reversed(range(1, n_ctx)):
            when_reducer(ctx_peers[d], lambda: rs_copy(p, d).start())

    def reduce(p):
        def body():
            for d in range(1, n_ctx):
                rs_copy(p, d).wait_recv()
            for j in range(half):
                total = rs_out[p, c, j].astype(F32)
                for d in range(1, n_ctx):
                    total = total + rs_in[p, d, j].astype(F32)
                ag_out[p, j] = total.astype(BF16)
            for d in reversed(range(1, n_ctx)):
                ag_copy(p, d, c).start()
            own_copy(p).start()

        when_reducer(c, body)

    def collect(p):
        for d in range(1, n_ctx):
            when_reducer(
                ctx_peers[d], lambda: ag_copy(p, d, ctx_peers[d]).wait_recv()
            )

    for e in direct[1:]:
        arrived(e)
        there = slot(fsdp_peers[e])
        dk_copies[e + 1] = remote(
            there, there, dk_s.at[e + 1], dk_r.at[e + 1], (c, fsdp_peers[1])
        )
        dk_copies[e + 1].start()
    spread(0)
    arrived(1)
    for e in direct[1:]:
        arrived(e + 1)
    spread(1)
    reduce(0)
    reduce(1)
    collect(0)
    collect(1)

    for d in range(1, n_ctx):
        for p in range(2):
            when_reducer(ctx_peers[d], lambda: rs_copy(p, d).wait_send())
            when_reducer(c, lambda: ag_copy(p, d, c).wait_send())
        kv_copies[d].wait_send()
        pk_copies[d].wait_send()
        pv_copies[d].wait_send()
    for e in dk_copies:
        dk_copies[e].wait_send()
    for write in writes:
        write.wait()
    for p in range(2):
        when_reducer(c, lambda: own_copy(p).wait())


def write_out(*refs):
    sources, targets, held = refs[:4], refs[4:8], refs[8:12]
    wide, in_s, out_s = refs[12:]
    loads = [pltpu.make_async_copy(sources[i], held[i], in_s.at[i]) for i in range(4)]
    stores = [
        pltpu.make_async_copy(wide if i == 3 else held[i], targets[i], out_s.at[i])
        for i in range(4)
    ]
    for i in (3, 0, 1, 2):
        loads[i].start()
    for i in range(3):
        loads[i].wait()
        stores[i].start()
    loads[3].wait()
    for group in range(HEAD_GROUPS):
        columns = slice(group * HEAD_SIZE, (group + 1) * HEAD_SIZE)
        wide[:, columns] = held[3][group % 2, group // 2].astype(F32)
    stores[3].start()
    for store in stores:
        store.wait()


def local(
    n_ctx, n_fsdp, block_pos, queries, keys, values, output, output_gradient, norm, features
):
    rows = keys.shape[1]
    seqs, _, cols = features.shape
    heads = queries.shape[2] // HEAD_SIZE
    total = HEAD_GROUPS * keys.shape[2]
    reducers = max(r for r in range(1, n_ctx + 1) if cols % (16 * r) == 0)
    part = cols // reducers
    half = HEAD_GROUPS // 2
    hbm = pl.BlockSpec(memory_space=pltpu.HBM)
    dma = pltpu.SemaphoreType.DMA
    shapes = (
        jax.ShapeDtypeStruct(queries.shape, BF16),
        jax.ShapeDtypeStruct(keys.shape, BF16),
        jax.ShapeDtypeStruct(keys.shape, BF16),
        jax.ShapeDtypeStruct((2, half, cols, HEAD_SIZE), BF16),
    )
    results = pl.pallas_call(
        functools.partial(kernel, n_ctx, n_fsdp, reducers),
        out_shape=shapes,
        in_specs=[hbm] * 8,
        out_specs=(hbm,) * 4,
        scratch_shapes=[
            pltpu.VMEM((n_ctx, 2 * rows + PLACE_ROWS, HEAD_SIZE), BF16),
            pltpu.VMEM((heads * rows, HEAD_SIZE), BF16),
            pltpu.VMEM((heads * rows, HEAD_SIZE), BF16),
            pltpu.VMEM((n_ctx * rows, heads * rows), BF16),
            pltpu.VMEM((n_ctx, rows, HEAD_SIZE), BF16),
            pltpu.VMEM((n_ctx, rows, HEAD_SIZE), BF16),
            pltpu.VMEM((n_ctx, rows, HEAD_SIZE), BF16),
            pltpu.VMEM((n_ctx, rows, HEAD_SIZE), BF16),
            pltpu.VMEM((rows, HEAD_SIZE), F32),
            pltpu.VMEM((rows, HEAD_SIZE), F32),
            pltpu.VMEM((HEAD_GROUPS, seqs * rows, HEAD_SIZE), BF16),
            pltpu.VMEM((cols, seqs * rows), BF16),
            pltpu.VMEM((2, n_ctx, half, part, HEAD_SIZE), BF16),
            pltpu.VMEM((2, n_ctx, half, part, HEAD_SIZE), BF16),
            pltpu.VMEM((2, half, part, HEAD_SIZE), BF16),
        ]
        + [dma((n_ctx,))] * 6
        + [dma((n_fsdp,))] * 2
        + [dma((2 * n_ctx,))] * 4
        + [
            pltpu.SMEM((1, seqs), jnp.int32),
            pltpu.VMEM(queries.shape[1:], BF16),
            pltpu.VMEM(queries.shape[1:], BF16),
            pltpu.VMEM(queries.shape[1:], BF16),
            pltpu.VMEM((heads, 1, rows), F32),
            dma((7 + seqs,)),
            pltpu.VMEM(queries.shape, BF16),
            pltpu.VMEM(keys.shape, BF16),
            pltpu.VMEM(keys.shape, BF16),
            pltpu.VMEM((n_ctx * rows, heads * rows), BF16),
            dma((5,)),
        ],
        compiler_params=pltpu.CompilerParams(
            collective_id=0, has_side_effects=True, vmem_limit_bytes=60 * 1024 * 1024
        ),
    )(
        block_pos.T,
        queries,
        keys,
        values,
        output,
        output_gradient,
        jnp.swapaxes(norm, 0, 1),
        jnp.swapaxes(features, 1, 2),
    )
    return pl.pallas_call(
        write_out,
        out_shape=(*shapes[:3], jax.ShapeDtypeStruct((cols, total), F32)),
        in_specs=[hbm] * 4,
        out_specs=(hbm,) * 4,
        scratch_shapes=[pltpu.VMEM(each.shape, each.dtype) for each in shapes]
        + [pltpu.VMEM((cols, total), F32), dma((4,)), dma((4,))],
    )(*results)


def solution(mesh):
    return jax.shard_map(
        functools.partial(local, mesh.shape["ctx"], mesh.shape["fsdp"]),
        mesh=mesh,
        in_specs=(
            P(None, "ctx"),
            P("fsdp", "ctx", None),
            P("fsdp", "ctx", None),
            P("fsdp", "ctx", None),
            P("fsdp", "ctx", None),
            P("fsdp", "ctx", None),
            P("fsdp", None, "ctx"),
            P(None, "ctx", "fsdp"),
        ),
        out_specs=(
            P("fsdp", "ctx", None),
            P("fsdp", "ctx", None),
            P("fsdp", "ctx", None),
            P("fsdp", None),
        ),
        check_vma=False,
    )
```
